32 devices in a mesh: row: 4 (over x, core), col: 8 (over z, y).
Axes of the slice: x: 2, y: 2, z: 4, core: 2. Of those that a mesh axis runs over, the one named last changes fastest.
Arguments:
- left_factor: bfloat16 [8, 1024, 48, 2048], P(None, 'row', None, 'col'), may hold values from -0.01953125 to 0.01953125
- prev_solution: bfloat16 [48, 2048, 512], P('row', 'col'), may hold values from -6 to 6
- cross: bfloat16 [8, 1024, 512], P(None, 'row'), may hold values from -6 to 6
- inverses: bfloat16 [2, 4, 1024, 2, 2048], P(None, None, 'row', None, 'col'), as said below
- coupling: bfloat16 [4, 1024, 2, 2048], P(None, 'row', None, 'col'), may hold values from -0.09375 to 0.09375
- prior_cov: float32 [512, 512], P('col'), may hold values from -6 to 6
Outputs:
- solved: bfloat16 [8, 1024, 512], P(None, 'row')
- pred_cov: float32 [512, 512], P('col')
The draws below stay inside these ranges and needn't reach their ends.
Inputs may be any that keep to these rules, and one draw needn't show every extreme that they name: Each block of inverses is lower triangular in natural order, with diagonal entries from 0.5 to 1.5.
All inputs are finite; a program needn't handle non-finite values.
Results may differ from the reference program's by a relative error of at most 0.0056.
Values may be sent and summed in bfloat16 or wider, within the bound.
A program may use at most 128 MiB of HBM per device.

```python
import jax
import jax.numpy as jnp

TB = 256
S = 8192
P_SIZE = 98304
M = 512
PANEL = 4096
N_ROW = 4
N_COL = 8


def draw_inverses(key, part):
    key_off = jax.random.fold_in(key, 11)
    key_diag = jax.random.fold_in(key, 12)
    rows = jnp.arange(PANEL)[:, None]
    cols = jnp.arange(PANEL)[None, :]
    lower = (cols < rows).astype(jnp.float32)
    eye = (cols == rows).astype(jnp.float32)
    off_part = jax.random.normal(key_off, (2, PANEL, PANEL), jnp.float32) * (0.6 / PANEL ** 0.5)
    diag_part = jax.random.uniform(key_diag, (2, PANEL, 1), jnp.float32, 0.6, 1.4)
    whole = off_part * lower + diag_part * eye
    return whole.reshape(2, PANEL // (N_ROW * TB), N_ROW * TB, PANEL // (N_COL * TB), N_COL * TB).astype(jnp.bfloat16)


def block_scale(stream_key, extent, cuts, least, largest):
    factor_of, own = 1.0, jax.random.fold_in(stream_key, 6)
    for position, parts in cuts:
        draws = jnp.exp(jax.random.uniform(jax.random.fold_in(own, position), (parts,), jnp.float32, least / len(cuts), largest / len(cuts)))
        factor_of = factor_of * jnp.repeat(draws, extent[position] // parts).reshape([-1 if axis == position else 1 for axis in range(len(extent))])
    return factor_of


def centred(stream_key, extent, spread, limit, pieces=(), held_as=jnp.bfloat16):
    array = spread * jax.random.normal(stream_key, extent, jnp.float32)
    if pieces:
        array = array * block_scale(stream_key, extent, pieces, -0.22, 0.18)
    return jnp.clip(array, -limit, limit).astype(held_as)


def setup_inputs(seed: int = 0) -> dict:
    key_of = jax.random.split(jax.random.key(seed), 7)
    left_factor = centred(key_of[0], (S // (N_ROW * TB), N_ROW * TB, P_SIZE // (N_COL * TB), N_COL * TB), P_SIZE ** -0.5, 0.01953125, ((1, 4), (3, 8)))
    prev_solution = centred(key_of[1], (P_SIZE // (N_COL * TB), N_COL * TB, M), 1.0, 6.0, ((0, 4), (1, 8)))
    cross = centred(key_of[2], (S // (N_ROW * TB), N_ROW * TB, M), 1.0, 6.0, ((1, 4),))
    inverses = draw_inverses(jax.random.fold_in(key_of[6], 71), 0)
    coupling = centred(key_of[4], (PANEL // (N_ROW * TB), N_ROW * TB, PANEL // (N_COL * TB), N_COL * TB), PANEL ** -0.5, 0.09375, ((1, 4), (3, 8)))
    prior_cov = centred(key_of[5], (M, M), 1.0, 6.0, ((0, 8),), jnp.float32)
    return dict(left_factor=left_factor, prev_solution=prev_solution, cross=cross, inverses=inverses, coupling=coupling, prior_cov=prior_cov)


def reference(left_factor, prev_solution, cross, inverses, coupling, prior_cov):
    left_whole = left_factor.reshape(S, P_SIZE)
    prev_whole = prev_solution.reshape(P_SIZE, M)
    cross_whole = cross.reshape(S, M).astype(jnp.float32)
    first_inv = inverses[0].reshape(PANEL, PANEL)
    second_inv = inverses[1].reshape(PANEL, PANEL)
    coupled = coupling.reshape(PANEL, PANEL)
    pre = jnp.dot(left_whole, prev_whole, preferred_element_type=jnp.float32)
    first_rhs = (cross_whole[:PANEL] - pre[:PANEL]).astype(jnp.bfloat16)
    solved_first = jnp.dot(first_inv, first_rhs, preferred_element_type=jnp.float32).astype(jnp.bfloat16)
    linked = jnp.dot(coupled, solved_first, preferred_element_type=jnp.float32)
    second_rhs = (cross_whole[PANEL:] - pre[PANEL:] - linked).astype(jnp.bfloat16)
    solved_second = jnp.dot(second_inv, second_rhs, preferred_element_type=jnp.float32).astype(jnp.bfloat16)
    solved_all = jnp.concatenate([solved_first, solved_second], axis=0)
    outer = jnp.dot(solved_all.T, solved_all, preferred_element_type=jnp.float32)
    pred_cov = prior_cov - outer / S
    return solved_all.reshape(S // (N_ROW * TB), N_ROW * TB, M), pred_cov
```

```python
import functools

import jax
import jax.numpy as jnp
from jax import lax
from jax.experimental import pallas as pl
from jax.experimental.pallas import tpu as pltpu
from jax.sharding import PartitionSpec as P

F32, BF16 = jnp.float32, jnp.bfloat16
PIECES = 2
MESH = pl.DeviceIdType.MESH


def chain_kernel(
    n_row, n_col, total_rows,
    pre_ref, cross_ref, gown_ref, gpair_ref, prior_ref,
    out_ref, cov_ref,
    part, second, stage, land, rhs, sol, pair_out, pair_in, cov_out, cov_in, cov_all,
    s_pair, r_pair, s_red, r_red, s_x, r_x, s_core, r_core,
    s_gat, r_gat, s_fwd, r_fwd, s_cov, r_cov,
):
    tiles, tile, sites = pre_ref.shape
    half = tiles // 2
    n_z = n_col // 2
    owners = n_col // n_row
    per = half // owners
    mh = sites // 2
    width = mh // PIECES
    band = n_row // 2

    row, col = lax.axis_index("row"), lax.axis_index("col")
    z, y = col // 2, col % 2
    core = row % 2
    mate_col = col + 1 - 2 * y
    mate_row = row + 1 - 2 * core
    mine = z // band
    active = z % band == row // 2

    def remote(src, dst, send, recv, r, c):
        return pltpu.make_async_remote_copy(
            src_ref=src, dst_ref=dst, send_sem=send, recv_sem=recv,
            device_id={"row": r, "col": c}, device_id_type=MESH)

    barrier = pltpu.get_barrier_semaphore()
    count = 1
    pl.semaphore_signal(barrier, inc=1, device_id={"row": row, "col": mate_col}, device_id_type=MESH)
    for dr in range(n_row):
        for dz in range(n_z):
            if dr or dz:
                count += 1
                pl.semaphore_signal(
                    barrier, inc=1,
                    device_id={"row": (row + dr) % n_row, "col": ((z + dz) % n_z) * 2 + y},
                    device_id_type=MESH)
    pl.semaphore_wait(barrier, count)

    def lanes(h, p):
        return pl.ds(pl.multiple_of(h * mh + p * width, 128), width)

    def pair_copy(panel, p):
        return remote(pair_out.at[panel, p], pair_in.at[panel, p], s_pair.at[panel, p], r_pair.at[panel, p], row, mate_col)

    for panel in range(2):
        for p in range(PIECES):
            for a in range(half):
                pair_out[panel, p, a] = pre_ref[panel * half + a, :, lanes(1 - y, p)].astype(BF16)
            pair_copy(panel, p).start()

    def pair_sum(panel, p, a):
        return pre_ref[panel * half + a, :, lanes(y, p)] + pair_in[panel, p, a].astype(F32)

    def reduce_copy(f, p, i):
        owner_z = i * band + row // 2
        slot = (z - owner_z + n_z) % n_z - 1
        return remote(stage.at[f, p, i], land.at[f, p, slot], s_red.at[f, p, i], r_red.at[f, p, slot], row, owner_z * 2 + y)

    def not_owner(i):
        return z != i * band + row // 2

    def send_parts(f, p):
        for i in range(owners):
            for k in range(per):
                stage[f, p, i, k] = part[p, i + owners * k].astype(BF16)

            @pl.when(not_owner(i))
            def _():
                reduce_copy(f, p, i).start()

    def wait_landed(f, p, slot):
        remote(land.at[f, p, slot], land.at[f, p, slot], s_red.at[f, p, 0], r_red.at[f, p, slot], row, mate_col).wait_recv()

    def x_copy(f, p, j):
        peer = (row + 2 * j) % n_row
        return remote(rhs.at[f, p, core], rhs.at[f, p, core], s_x.at[f, p, j - 1], r_x.at[f, p], peer, col)

    def core_copy(f, p):
        return remote(rhs.at[f, p, core], rhs.at[f, p, core], s_core.at[f, p], r_core.at[f, p], mate_row, col)

    def core_wait(f, p):
        remote(rhs.at[f, p, 1 - core], rhs.at[f, p, 1 - core], s_core.at[f, p], r_core.at[f, p], mate_row, col).wait_recv()

    def gather_copy(g, p, dz):
        return remote(sol.at[y, g, p, mine], sol.at[y, g, p, mine], s_gat.at[g, p, dz - 1], r_gat.at[g, p, mine], row, ((z + dz) % n_z) * 2 + y)

    def forward_copy(g, p, i):
        return remote(sol.at[y, g, p, i], sol.at[y, g, p, i], s_fwd.at[g, p, i], r_fwd.at[g, p, i], row, mate_col)

    def take(f, p):
        @pl.when(active)
        def _():
            for slot in range(n_z - 1):
                wait_landed(f, p, slot)
            for k in range(per):
                total = part[p, mine + owners * k]
                for slot in range(n_z - 1):
                    total = total + land[f, p, slot, k].astype(F32)
                if f % 2 == 0:
                    total = cross_ref[(f // 2) * half + mine + owners * k, :, lanes(y, p)].astype(F32) - total
                value = total.astype(BF16)
                if f < 3:
                    rhs[f, p, core, k] = value
                if f % 2 == 1:
                    sol[y, f // 2, p, mine, k] = value
            if f < 3:
                for j in range(1, band):
                    x_copy(f, p, j).start()
            if f % 2 == 1:
                for dz in range(1, n_z):
                    gather_copy(f // 2, p, dz).start()

        if f < 3:
            @pl.when(jnp.logical_not(active))
            def _():
                remote(rhs.at[f, p, core], rhs.at[f, p, core], s_core.at[f, p], r_x.at[f, p], mate_row, col).wait_recv()
            core_copy(f, p).start()
            core_wait(f, p)

    def apply(f, p):
        near = rhs[f - 1, p, y].reshape(per * tile, width)
        far = rhs[f - 1, p, 1 - y].reshape(per * tile, width)
        for a in range(half):
            rows = pl.ds(a * tile, tile)
            got = jnp.dot(gown_ref[f - 1, rows, :], near, preferred_element_type=F32)
            got = got + jnp.dot(gpair_ref[f - 1, rows, :], far, preferred_element_type=F32)
            if f == 2:
                got = got + second[p, a]
            part[p, a] = got

    def gather_on(g, p):
        for i in range(owners):
            @pl.when(not_owner(i))
            def _():
                remote(sol.at[y, g, p, i], sol.at[y, g, p, i], s_fwd.at[g, p, i], r_gat.at[g, p, i], row, mate_col).wait_recv()
            forward_copy(g, p, i).start()

    def gather_end(g, p):
        for i in range(owners):
            remote(sol.at[1 - y, g, p, i], sol.at[1 - y, g, p, i], s_fwd.at[g, p, i], r_fwd.at[g, p, i], row, mate_col).wait_recv()
        for h in range(2):
            for i in range(owners):
                for k in range(per):
                    out_ref[g * half + i + owners * k, :, pl.ds(h * mh + p * width, width)] = sol[h, g, p, i, k]

    share = prior_ref.shape[0]
    block = pl.multiple_of(col * share // 128 * 128, 128)

    def outer(g):
        rows = half * tile
        own = out_ref[pl.ds(g * half, half), :, pl.ds(block, 128)].reshape(rows, 128)
        every = out_ref[pl.ds(g * half, half)].reshape(rows, sites)
        return lax.dot_general(own, every, (((0,), (0,)), ((), ())), preferred_element_type=F32)

    for p in range(PIECES):
        pair_copy(0, p).wait_recv()
        for a in range(half):
            part[p, a] = pair_sum(0, p, a)
        send_parts(0, p)
    for p in range(PIECES):
        pair_copy(1, p).wait_recv()
        for a in range(half):
            second[p, a] = pair_sum(1, p, a)
    for f in range(4):
        for p in range(PIECES):
            take(f, p)
            if f < 3:
                apply(f + 1, p)
                send_parts(f + 1, p)
            if f == 2:
                gather_on(0, p)
    for p in range(PIECES):
        gather_end(0, p)
    cov_all[...] = outer(0)
    for p in range(PIECES):
        gather_on(1, p)
    for p in range(PIECES):
        gather_end(1, p)
    cov_all[...] += outer(1)

    rows = pl.ds(pl.multiple_of(col * share % 128, share), share)
    own_cov = cov_all[rows, :]
    cov_out[...] = own_cov.astype(BF16)

    def cov_copy(j):
        return remote(cov_out, cov_in.at[j - 1], s_cov.at[j - 1], r_cov.at[j - 1], (row + j) % n_row, col)

    for j in range(1, n_row):
        cov_copy(j).start()
    total = own_cov
    for j in range(1, n_row):
        cov_copy(j).wait_recv()
        total = total + cov_in[j - 1].astype(F32)
    cov_ref[...] = prior_ref[...] - total / total_rows

    for j in range(1, n_row):
        cov_copy(j).wait_send()
    for p in range(PIECES):
        for panel in range(2):
            pair_copy(panel, p).wait_send()
            for i in range(owners):
                forward_copy(panel, p, i).wait_send()
        for f in range(4):
            for i in range(owners):
                @pl.when(not_owner(i))
                def _():
                    reduce_copy(f, p, i).wait_send()
            if f < 3:
                core_copy(f, p).wait_send()

        @pl.when(active)
        def _():
            for f in range(3):
                for j in range(1, band):
                    x_copy(f, p, j).wait_send()
            for g in range(2):
                for dz in range(1, n_z):
                    gather_copy(g, p, dz).wait_send()


def chain(n_row, n_col, pre, cross, gown, gpair, prior):
    tiles, tile, sites = pre.shape
    half, n_z, owners, band = tiles // 2, n_col // 2, n_col // n_row, n_row // 2
    per = half // owners
    width = sites // 2 // PIECES
    share = prior.shape[0]
    dma = pltpu.SemaphoreType.DMA
    vm = pl.BlockSpec(memory_space=pltpu.VMEM)
    return pl.pallas_call(
        functools.partial(chain_kernel, n_row, n_col, tiles * tile * n_row),
        out_shape=(
            jax.ShapeDtypeStruct((tiles, tile, sites), BF16),
            jax.ShapeDtypeStruct((share, sites), F32),
        ),
        in_specs=[vm] * 5,
        out_specs=(vm, vm),
        scratch_shapes=[
            pltpu.VMEM((PIECES, half, tile, width), F32),
            pltpu.VMEM((PIECES, half, tile, width), F32),
            pltpu.VMEM((4, PIECES, owners, per, tile, width), BF16),
            pltpu.VMEM((4, PIECES, n_z - 1, per, tile, width), BF16),
            pltpu.VMEM((3, PIECES, 2, per, tile, width), BF16),
            pltpu.VMEM((2, 2, PIECES, owners, per, tile, width), BF16),
            pltpu.VMEM((2, PIECES, half, tile, width), BF16),
            pltpu.VMEM((2, PIECES, half, tile, width), BF16),
            pltpu.VMEM((share, sites), BF16),
            pltpu.VMEM((n_row - 1, share, sites), BF16),
            pltpu.VMEM((128, sites), F32),
            dma((2, PIECES)), dma((2, PIECES)),
            dma((4, PIECES, owners)), dma((4, PIECES, n_z - 1)),
            dma((3, PIECES, max(band - 1, 1))), dma((3, PIECES)),
            dma((3, PIECES)), dma((3, PIECES)),
            dma((2, PIECES, n_z - 1)), dma((2, PIECES, owners)),
            dma((2, PIECES, owners)), dma((2, PIECES, owners)),
            dma((n_row - 1,)), dma((n_row - 1,)),
        ],
        compiler_params=pltpu.CompilerParams(
            collective_id=0, has_side_effects=True, vmem_limit_bytes=48 * 1024 * 1024),
    )(pre, cross, gown, gpair, prior)


def body(n_row, n_col, left_factor, prev_solution, cross, inverses, coupling, prior_cov):
    half, tile, cols, _ = coupling.shape
    blocks = jnp.stack([inverses[0], coupling, inverses[1]]).reshape(3, half * tile, cols * tile)
    mate = lax.ppermute(blocks, "col", [(c, c ^ 1) for c in range(n_col)])
    pre = jnp.einsum(
        "atbu,bum->atm",
        left_factor,
        lax.all_gather(prev_solution, "row", axis=0, tiled=True),
        preferred_element_type=F32,
    )
    return chain(n_row, n_col, pre, cross, blocks, mate, prior_cov)


def solution(mesh):
    placed = (
        P(None, "row", None, "col"),
        P("row", "col", None),
        P(None, "row", None),
        P(None, None, "row", None, "col"),
        P(None, "row", None, "col"),
        P("col", None),
    )
    return jax.shard_map(
        functools.partial(body, mesh.shape["row"], mesh.shape["col"]),
        mesh=mesh,
        in_specs=placed,
        out_specs=(P(None, "row", None), P("col", None)),
        check_vma=False,
    )
```

```python
import functools

import jax
import jax.numpy as jnp
from jax import lax
from jax.experimental import pallas as pl
from jax.experimental.pallas import tpu as pltpu
from jax.sharding import PartitionSpec as P

F32, BF16 = jnp.float32, jnp.bfloat16
PIECES = 2
MESH = pl.DeviceIdType.MESH


def chain_kernel(
    n_row, n_col, chunk, local, total_rows,
    left_ref, prev_ref, cross_ref, ginv_ref, gmid_ref, prior_ref,
    out_ref, cov_ref,
    pre_ref, solved_rows, left_buf, pinv, pmid, part, stage, land, rhs, sol, pair_out, pair_in, cov_out, cov_in, cov_all,
    s_pair, r_pair, s_red, r_red, s_x, r_x, s_core, r_core,
    s_gat, r_gat, s_fwd, r_fwd, s_cov, r_cov,
    l_own, l_left, s_vx, r_vx, s_vc, r_vc, s_g, r_g,
):
    tiles, tile, sites = pre_ref.shape
    half = tiles // 2
    n_z = n_col // 2
    owners = n_col // n_row
    per = half // owners
    mh = sites // 2
    width = mh // PIECES
    band = n_row // 2

    row, col = lax.axis_index("row"), lax.axis_index("col")
    z, y = col // 2, col % 2
    core = row % 2
    mate_col = col + 1 - 2 * y
    mate_row = row + 1 - 2 * core
    mine = z // band
    active = z % band == row // 2

    def remote(src, dst, send, recv, r, c):
        return pltpu.make_async_remote_copy(
            src_ref=src, dst_ref=dst, send_sem=send, recv_sem=recv,
            device_id={"row": r, "col": c}, device_id_type=MESH)

    held = prev_ref.shape[0]
    rounds = left_ref.shape[2]
    wide = 2 * width

    def own_copy(p):
        return pltpu.make_async_copy(
            prev_ref.at[:, :, pl.ds(p * wide, wide)],
            solved_rows.at[p, pl.ds(row * held, held)], l_own.at[p])

    for p in range(PIECES):
        own_copy(p).start()

    barrier = pltpu.get_barrier_semaphore()
    count = 1
    pl.semaphore_signal(barrier, inc=1, device_id={"row": row, "col": mate_col}, device_id_type=MESH)
    for dr in range(n_row):
        for dz in range(n_z):
            if dr or dz:
                count += 1
                pl.semaphore_signal(
                    barrier, inc=1,
                    device_id={"row": (row + dr) % n_row, "col": ((z + dz) % n_z) * 2 + y},
                    device_id_type=MESH)
    pl.semaphore_wait(barrier, count)

    def lanes(h, p):
        return pl.ds(pl.multiple_of(p * wide + h * width, 128), width)

    def pair_copy(panel, p):
        return remote(pair_out.at[panel, p], pair_in.at[panel, p], s_pair.at[panel, p], r_pair.at[panel, p], row, mate_col)

    def pair_start(p):
        for panel in range(2):
            for a in range(half):
                pair_out[panel, p, a] = pre_ref[panel * half + a, :, lanes(1 - y, p)].astype(BF16)
            pair_copy(panel, p).start()

    def pair_sum(panel, p, a):
        return pre_ref[panel * half + a, :, lanes(y, p)] + pair_in[panel, p, a].astype(F32)

    def reduce_copy(f, p, i):
        owner_z = i * band + row // 2
        slot = (z - owner_z + n_z) % n_z - 1
        return remote(stage.at[f, p, i], land.at[f, p, slot], s_red.at[f, p, i], r_red.at[f, p, slot], row, owner_z * 2 + y)

    def not_owner(i):
        return z != i * band + row // 2

    def send_parts(f, p):
        for i in range(owners):
            for k in range(per):
                stage[f, p, i, k] = part[p, i + owners * k].astype(BF16)

            @pl.when(not_owner(i))
            def _():
                reduce_copy(f, p, i).start()

    def wait_landed(f, p, slot):
        remote(land.at[f, p, slot], land.at[f, p, slot], s_red.at[f, p, 0], r_red.at[f, p, slot], row, mate_col).wait_recv()

    def x_copy(f, p, j):
        peer = (row + 2 * j) % n_row
        return remote(rhs.at[f, p, core], rhs.at[f, p, core], s_x.at[f, p, j - 1], r_x.at[f, p], peer, col)

    def core_copy(f, p):
        return remote(rhs.at[f, p, core], rhs.at[f, p, core], s_core.at[f, p], r_core.at[f, p], mate_row, col)

    def core_wait(f, p):
        remote(rhs.at[f, p, 1 - core], rhs.at[f, p, 1 - core], s_core.at[f, p], r_core.at[f, p], mate_row, col).wait_recv()

    def gather_copy(g, p, dz):
        return remote(sol.at[y, g, p, mine], sol.at[y, g, p, mine], s_gat.at[g, p, dz - 1], r_gat.at[g, p, mine], row, ((z + dz) % n_z) * 2 + y)

    def forward_copy(g, p, i):
        return remote(sol.at[y, g, p, i], sol.at[y, g, p, i], s_fwd.at[g, p, i], r_fwd.at[g, p, i], row, mate_col)

    def take(f, p):
        @pl.when(active)
        def _():
            for slot in range(n_z - 1):
                wait_landed(f, p, slot)
            for k in range(per):
                total = part[p, mine + owners * k]
                for slot in range(n_z - 1):
                    total = total + land[f, p, slot, k].astype(F32)
                if f % 2 == 0:
                    total = cross_ref[(f // 2) * half + mine + owners * k, :, lanes(y, p)].astype(F32) - total
                value = total.astype(BF16)
                if f < 3:
                    rhs[f, p, core, k] = value
                if f % 2 == 1:
                    sol[y, f // 2, p, mine, k] = value
            if f < 3:
                for j in range(1, band):
                    x_copy(f, p, j).start()
            if f % 2 == 1:
                for dz in range(1, n_z):
                    gather_copy(f // 2, p, dz).start()

        if f < 3:
            @pl.when(jnp.logical_not(active))
            def _():
                remote(rhs.at[f, p, core], rhs.at[f, p, core], s_core.at[f, p], r_x.at[f, p], mate_row, col).wait_recv()
            core_copy(f, p).start()
            core_wait(f, p)

    def apply(f, p):
        near = rhs[f - 1, p, y].reshape(per * tile, width)
        far = rhs[f - 1, p, 1 - y].reshape(per * tile, width)
        if f == 2:
            pair_copy(1, p).wait_recv()
        if p == 0:
            block_copy(f - 1).wait_recv()
        for a in range(half):
            rows = pl.ds(a * tile, tile)
            here = gmid_ref[rows, :] if f == 2 else ginv_ref[f // 2, rows, :]
            there = pmid[rows, :] if f == 2 else pinv[f // 2, rows, :]
            got = jnp.dot(here, near, preferred_element_type=F32)
            got = got + jnp.dot(there, far, preferred_element_type=F32)
            if f == 2:
                got = got + pair_sum(1, p, a)
            part[p, a] = got

    def gather_on(g, p):
        for i in range(owners):
            @pl.when(not_owner(i))
            def _():
                remote(sol.at[y, g, p, i], sol.at[y, g, p, i], s_fwd.at[g, p, i], r_gat.at[g, p, i], row, mate_col).wait_recv()
            forward_copy(g, p, i).start()

    def gather_end(g, p):
        for i in range(owners):
            remote(sol.at[1 - y, g, p, i], sol.at[1 - y, g, p, i], s_fwd.at[g, p, i], r_fwd.at[g, p, i], row, mate_col).wait_recv()
        for h in range(2):
            for i in range(owners):
                for k in range(per):
                    out_ref[g * half + i + owners * k, :, pl.ds(p * wide + h * width, width)] = sol[h, g, p, i, k]

    share = prior_ref.shape[0]
    block = pl.multiple_of(col * share // 128 * 128, 128)

    def outer(g):
        rows = half * tile
        own = out_ref[pl.ds(g * half, half), :, pl.ds(block, 128)].reshape(rows, 128)
        every = out_ref[pl.ds(g * half, half)].reshape(rows, sites)
        return lax.dot_general(own, every, (((0,), (0,)), ((), ())), preferred_element_type=F32)

    def rows_of(p, r):
        return solved_rows.at[p, pl.ds(r * held, held)]

    def cross_copy(p, j):
        return remote(rows_of(p, row), rows_of(p, row), s_vx.at[p, j - 1], r_vx.at[p, j - 1], (row + 2 * j) % n_row, col)

    def cross_wait(p, j):
        src = rows_of(p, (row + n_row - 2 * j) % n_row)
        remote(src, src, s_vx.at[p, j - 1], r_vx.at[p, j - 1], mate_row, col).wait_recv()

    def hand_copy(p, j):
        src = rows_of(p, (row + n_row - 2 * j) % n_row)
        return remote(src, src, s_vc.at[p, j], r_vc.at[p, j], mate_row, col)

    def hand_wait(p, j):
        src = rows_of(p, (mate_row + n_row - 2 * j) % n_row)
        remote(src, src, s_vc.at[p, j], r_vc.at[p, j], mate_row, col).wait_recv()

    def block_copy(n):
        src = gmid_ref if n == 1 else ginv_ref.at[n // 2]
        dst = pmid if n == 1 else pinv.at[n // 2]
        return remote(src, dst, s_g.at[n], r_g.at[n], row, mate_col)

    def product(first, chunks, pieces, fresh):
        steps = tiles * chunks

        def fetch(s, slot):
            at = pl.multiple_of((first + s % chunks) * chunk, chunk)
            return pltpu.make_async_copy(left_ref.at[s // chunks, :, pl.ds(at, chunk), :], left_buf.at[slot], l_left.at[slot])

        fetch(0, 0).start()

        def step(s, carry):
            slot = s % 2

            @pl.when(s + 1 < steps)
            def _():
                fetch(s + 1, 1 - slot).start()

            fetch(s, slot).wait()
            at = (first + s % chunks) * chunk
            block = left_buf[slot].reshape(tile, chunk * tile)
            for p in pieces:
                values = solved_rows[p, pl.ds(at, chunk)].reshape(chunk * tile, wide)
                got = jnp.dot(block, values, preferred_element_type=F32)
                where = (s // chunks, slice(None), pl.ds(p * wide, wide))
                if fresh:
                    pre_ref[where] = got
                else:
                    pre_ref[where] += got
            return carry

        lax.fori_loop(0, steps, step, 0)

    def bring(p):
        for j in range(1, band):
            cross_wait(p, j)
            hand_copy(p, j).start()
        if p + 1 < PIECES:
            for j in range(1, band):
                cross_copy(p, j).wait_send()
            for j in range(1, band):
                cross_copy(p + 1, j).start()
        for j in range(1, band):
            hand_wait(p, j)

    def rest(p):
        if local:
            product((1 - row // 2), rounds // chunk - 1, (p,), False)
        else:
            for n in range(rounds // chunk):
                product(n, 1, (p,), n == 0)

    def first_sum(p):
        pair_copy(0, p).wait_recv()
        for a in range(half):
            part[p, a] = pair_sum(0, p, a)
        send_parts(0, p)

    def advance(f, p):
        take(f, p)
        if f < 3:
            apply(f + 1, p)
            send_parts(f + 1, p)

    for p in range(PIECES):
        own_copy(p).wait()
        hand_copy(p, 0).start()
        if p == 0:
            for j in range(1, band):
                cross_copy(p, j).start()
    for n in range(3):
        block_copy(n).start()
    for p in range(PIECES):
        hand_wait(p, 0)
    if local:
        product((row // 2) * (rounds // chunk - 1), 1, tuple(range(PIECES)), True)
    bring(0)
    rest(0)
    pair_start(0)
    first_sum(0)
    advance(0, 0)
    bring(1)
    rest(1)
    pair_start(1)
    advance(1, 0)
    first_sum(1)
    advance(2, 0)
    advance(0, 1)
    advance(3, 0)
    advance(1, 1)
    gather_on(0, 0)
    advance(2, 1)
    gather_on(0, 1)
    gather_on(1, 0)
    gather_end(0, 0)
    gather_end(1, 0)
    advance(3, 1)
    gather_end(0, 1)
    cov_all[...] = outer(0)
    gather_on(1, 1)
    gather_end(1, 1)
    cov_all[...] += outer(1)

    rows = pl.ds(pl.multiple_of(col * share % 128, share), share)
    own_cov = cov_all[rows, :]
    cov_out[...] = own_cov.astype(BF16)

    def cov_copy(j):
        return remote(cov_out, cov_in.at[j - 1], s_cov.at[j - 1], r_cov.at[j - 1], (row + j) % n_row, col)

    for j in range(1, n_row):
        cov_copy(j).start()
    total = own_cov
    for j in range(1, n_row):
        cov_copy(j).wait_recv()
        total = total + cov_in[j - 1].astype(F32)
    cov_ref[...] = prior_ref[...] - total / total_rows

    for j in range(1, n_row):
        cov_copy(j).wait_send()
    for n in range(3):
        block_copy(n).wait_send()
    for j in range(1, band):
        cross_copy(PIECES - 1, j).wait_send()
    for p in range(PIECES):
        for j in range(band):
            hand_copy(p, j).wait_send()
    for p in range(PIECES):
        for panel in range(2):
            pair_copy(panel, p).wait_send()
            for i in range(owners):
                forward_copy(panel, p, i).wait_send()
        for f in range(4):
            for i in range(owners):
                @pl.when(not_owner(i))
                def _():
                    reduce_copy(f, p, i).wait_send()
            if f < 3:
                core_copy(f, p).wait_send()

        @pl.when(active)
        def _():
            for f in range(3):
                for j in range(1, band):
                    x_copy(f, p, j).wait_send()
            for g in range(2):
                for dz in range(1, n_z):
                    gather_copy(g, p, dz).wait_send()


def chain(n_row, n_col, left, prev, cross, inverses, coupling, prior):
    tiles, tile, rounds, _ = left.shape
    sites = prev.shape[2]
    half, n_z, owners, band = tiles // 2, n_col // 2, n_col // n_row, n_row // 2
    per = half // owners
    width = sites // 2 // PIECES
    share = prior.shape[0]
    local = band == 2 and rounds % 16 == 0 and rounds >= 32
    chunk = 16 if local else rounds
    dma = pltpu.SemaphoreType.DMA
    vm = pl.BlockSpec(memory_space=pltpu.VMEM)
    hbm = pl.BlockSpec(memory_space=pl.ANY)
    return pl.pallas_call(
        functools.partial(chain_kernel, n_row, n_col, chunk, local, tiles * tile * n_row),
        out_shape=(
            jax.ShapeDtypeStruct((tiles, tile, sites), BF16),
            jax.ShapeDtypeStruct((share, sites), F32),
        ),
        in_specs=[hbm, hbm] + [vm] * 4,
        out_specs=(vm, vm),
        scratch_shapes=[
            pltpu.VMEM((tiles, tile, sites), F32),
            pltpu.VMEM((PIECES, rounds, tile, 2 * width), BF16),
            pltpu.VMEM((2, tile, chunk, tile), BF16),
            pltpu.VMEM(inverses.shape, BF16),
            pltpu.VMEM(coupling.shape, BF16),
            pltpu.VMEM((PIECES, half, tile, width), F32),
            pltpu.VMEM((4, PIECES, owners, per, tile, width), BF16),
            pltpu.VMEM((4, PIECES, n_z - 1, per, tile, width), BF16),
            pltpu.VMEM((3, PIECES, 2, per, tile, width), BF16),
            pltpu.VMEM((2, 2, PIECES, owners, per, tile, width), BF16),
            pltpu.VMEM((2, PIECES, half, tile, width), BF16),
            pltpu.VMEM((2, PIECES, half, tile, width), BF16),
            pltpu.VMEM((share, sites), BF16),
            pltpu.VMEM((n_row - 1, share, sites), BF16),
            pltpu.VMEM((128, sites), F32),
            dma((2, PIECES)), dma((2, PIECES)),
            dma((4, PIECES, owners)), dma((4, PIECES, n_z - 1)),
            dma((3, PIECES, max(band - 1, 1))), dma((3, PIECES)),
            dma((3, PIECES)), dma((3, PIECES)),
            dma((2, PIECES, n_z - 1)), dma((2, PIECES, owners)),
            dma((2, PIECES, owners)), dma((2, PIECES, owners)),
            dma((n_row - 1,)), dma((n_row - 1,)),
            dma((PIECES,)), dma((2,)),
            dma((PIECES, max(band - 1, 1))), dma((PIECES, max(band - 1, 1))),
            dma((PIECES, band)), dma((PIECES, band)),
            dma((3,)), dma((3,)),
        ],
        compiler_params=pltpu.CompilerParams(
            collective_id=0, has_side_effects=True, vmem_limit_bytes=60 * 1024 * 1024),
    )(left, prev, cross, inverses, coupling, prior)


def body(n_row, n_col, left_factor, prev_solution, cross, inverses, coupling, prior_cov):
    half, tile, cols, _ = coupling.shape
    return chain(
        n_row, n_col, left_factor, prev_solution, cross,
        inverses.reshape(2, half * tile, cols * tile), coupling.reshape(half * tile, cols * tile), prior_cov)


def solution(mesh):
    placed = (
        P(None, "row", None, "col"),
        P("row", "col", None),
        P(None, "row", None),
        P(None, None, "row", None, "col"),
        P(None, "row", None, "col"),
        P("col", None),
    )
    return jax.shard_map(
        functools.partial(body, mesh.shape["row"], mesh.shape["col"]),
        mesh=mesh,
        in_specs=placed,
        out_specs=(P(None, "row", None), P("col", None)),
        check_vma=False,
    )
```

```python
import functools

import jax
import jax.numpy as jnp
from jax import lax
from jax.experimental import pallas as pl
from jax.experimental.pallas import tpu as pltpu
from jax.sharding import PartitionSpec as P

F32, BF16 = jnp.float32, jnp.bfloat16
PIECES = 2
MESH = pl.DeviceIdType.MESH


def chain_kernel(
    n_row, n_col, chunk, local, total_rows,
    left_ref, prev_ref, cross_ref, ginv_ref, gmid_ref, prior_ref,
    out_ref, cov_ref, flat_ref,
    pre_ref, solved_rows, left_buf, flat_buf, pinv, pmid, part, stage, land, rhs, sol, pair_out, pair_in, cov_out, cov_in, cov_all,
    s_pair, r_pair, s_red, r_red, s_x, r_x, s_core, r_core,
    s_gat, r_gat, s_fwd, r_fwd, s_cov, r_cov,
    l_own, l_left, l_flat, s_vx, r_vx, s_vc, r_vc, s_g, r_g,
):
    tiles, tile, sites = pre_ref.shape
    half = tiles // 2
    n_z = n_col // 2
    owners = n_col // n_row
    per = half // owners
    mh = sites // 2
    width = mh // PIECES
    band = n_row // 2

    row, col = lax.axis_index("row"), lax.axis_index("col")
    z, y = col // 2, col % 2
    core = row % 2
    mate_col = col + 1 - 2 * y
    mate_row = row + 1 - 2 * core
    mine = z // band
    active = z % band == row // 2

    def remote(src, dst, send, recv, r, c):
        return pltpu.make_async_remote_copy(
            src_ref=src, dst_ref=dst, send_sem=send, recv_sem=recv,
            device_id={"row": r, "col": c}, device_id_type=MESH)

    held = prev_ref.shape[0]
    rounds = left_ref.shape[2]
    wide = 2 * width

    def own_copy(p):
        return pltpu.make_async_copy(
            prev_ref.at[:, :, pl.ds(p * wide, wide)],
            solved_rows.at[p, pl.ds(row * held, held)], l_own.at[p])

    for p in range(PIECES):
        own_copy(p).start()

    barrier = pltpu.get_barrier_semaphore()
    count = 1
    pl.semaphore_signal(barrier, inc=1, device_id={"row": row, "col": mate_col}, device_id_type=MESH)
    for dr in range(n_row):
        for dz in range(n_z):
            if dr or dz:
                count += 1
                pl.semaphore_signal(
                    barrier, inc=1,
                    device_id={"row": (row + dr) % n_row, "col": ((z + dz) % n_z) * 2 + y},
                    device_id_type=MESH)
    pl.semaphore_wait(barrier, count)

    def lanes(h, p):
        return pl.ds(pl.multiple_of(p * wide + h * width, 128), width)

    def pair_copy(panel, p):
        return remote(pair_out.at[panel, p], pair_in.at[panel, p], s_pair.at[panel, p], r_pair.at[panel, p], row, mate_col)

    def pair_start(p):
        for panel in range(2):
            for a in range(half):
                pair_out[panel, p, a] = pre_ref[panel * half + a, :, lanes(1 - y, p)].astype(BF16)
            pair_copy(panel, p).start()

    def pair_sum(panel, p, a):
        return pre_ref[panel * half + a, :, lanes(y, p)] + pair_in[panel, p, a].astype(F32)

    def reduce_copy(f, p, i):
        owner_z = i * band + row // 2
        slot = (z - owner_z + n_z) % n_z - 1
        return remote(stage.at[f, p, i], land.at[f, p, slot], s_red.at[f, p, i], r_red.at[f, p, slot], row, owner_z * 2 + y)

    def not_owner(i):
        return z != i * band + row // 2

    def send_parts(f, p):
        for i in range(owners):
            for k in range(per):
                stage[f, p, i, k] = part[p, i + owners * k].astype(BF16)

            @pl.when(not_owner(i))
            def _():
                reduce_copy(f, p, i).start()

    def wait_landed(f, p, slot):
        remote(land.at[f, p, slot], land.at[f, p, slot], s_red.at[f, p, 0], r_red.at[f, p, slot], row, mate_col).wait_recv()

    def x_copy(f, p, j):
        peer = (row + 2 * j) % n_row
        return remote(rhs.at[f, p, core], rhs.at[f, p, core], s_x.at[f, p, j - 1], r_x.at[f, p], peer, col)

    def core_copy(f, p):
        return remote(rhs.at[f, p, core], rhs.at[f, p, core], s_core.at[f, p], r_core.at[f, p], mate_row, col)

    def core_wait(f, p):
        remote(rhs.at[f, p, 1 - core], rhs.at[f, p, 1 - core], s_core.at[f, p], r_core.at[f, p], mate_row, col).wait_recv()

    def gather_copy(g, p, dz):
        return remote(sol.at[y, g, p, mine], sol.at[y, g, p, mine], s_gat.at[g, p, dz - 1], r_gat.at[g, p, mine], row, ((z + dz) % n_z) * 2 + y)

    def forward_copy(g, p, i):
        return remote(sol.at[y, g, p, i], sol.at[y, g, p, i], s_fwd.at[g, p, i], r_fwd.at[g, p, i], row, mate_col)

    def take(f, p):
        @pl.when(active)
        def _():
            for slot in range(n_z - 1):
                wait_landed(f, p, slot)
            for k in range(per):
                total = part[p, mine + owners * k]
                for slot in range(n_z - 1):
                    total = total + land[f, p, slot, k].astype(F32)
                if f % 2 == 0:
                    total = cross_ref[(f // 2) * half + mine + owners * k, :, lanes(y, p)].astype(F32) - total
                value = total.astype(BF16)
                if f < 3:
                    rhs[f, p, core, k] = value
                if f % 2 == 1:
                    sol[y, f // 2, p, mine, k] = value
            if f < 3:
                for j in range(1, band):
                    x_copy(f, p, j).start()
            if f % 2 == 1:
                for dz in range(1, n_z):
                    gather_copy(f // 2, p, dz).start()

        if f < 3:
            @pl.when(jnp.logical_not(active))
            def _():
                remote(rhs.at[f, p, core], rhs.at[f, p, core], s_core.at[f, p], r_x.at[f, p], mate_row, col).wait_recv()
            core_copy(f, p).start()
            core_wait(f, p)

    def apply(f, p):
        near = rhs[f - 1, p, y].reshape(per * tile, width)
        far = rhs[f - 1, p, 1 - y].reshape(per * tile, width)
        if f == 2:
            pair_copy(1, p).wait_recv()
        if p == 0:
            block_copy(f - 1).wait_recv()
        for a in range(half):
            rows = pl.ds(a * tile, tile)
            here = gmid_ref[rows, :] if f == 2 else ginv_ref[f // 2, rows, :]
            there = pmid[rows, :] if f == 2 else pinv[f // 2, rows, :]
            got = jnp.dot(here, near, preferred_element_type=F32)
            got = got + jnp.dot(there, far, preferred_element_type=F32)
            if f == 2:
                got = got + pair_sum(1, p, a)
            part[p, a] = got

    def gather_on(g, p):
        for i in range(owners):
            @pl.when(not_owner(i))
            def _():
                remote(sol.at[y, g, p, i], sol.at[y, g, p, i], s_fwd.at[g, p, i], r_gat.at[g, p, i], row, mate_col).wait_recv()
            forward_copy(g, p, i).start()

    def gather_end(g, p):
        for i in range(owners):
            remote(sol.at[1 - y, g, p, i], sol.at[1 - y, g, p, i], s_fwd.at[g, p, i], r_fwd.at[g, p, i], row, mate_col).wait_recv()
        for h in range(2):
            for i in range(owners):
                for k in range(per):
                    out_ref[g * half + i + owners * k, :, pl.ds(p * wide + h * width, width)] = sol[h, g, p, i, k]

    share = prior_ref.shape[0]
    block = pl.multiple_of(col * share // 128 * 128, 128)

    def outer(g):
        rows = half * tile
        own = out_ref[pl.ds(g * half, half), :, pl.ds(block, 128)].reshape(rows, 128)
        every = out_ref[pl.ds(g * half, half)].reshape(rows, sites)
        return lax.dot_general(own, every, (((0,), (0,)), ((), ())), preferred_element_type=F32)

    def rows_of(p, r):
        return solved_rows.at[p, pl.ds(r * held, held)]

    def cross_copy(p, j):
        return remote(rows_of(p, row), rows_of(p, row), s_vx.at[p, j - 1], r_vx.at[p, j - 1], (row + 2 * j) % n_row, col)

    def cross_wait(p, j):
        src = rows_of(p, (row + n_row - 2 * j) % n_row)
        remote(src, src, s_vx.at[p, j - 1], r_vx.at[p, j - 1], mate_row, col).wait_recv()

    def hand_copy(p, j):
        src = rows_of(p, (row + n_row - 2 * j) % n_row)
        return remote(src, src, s_vc.at[p, j], r_vc.at[p, j], mate_row, col)

    def hand_wait(p, j):
        src = rows_of(p, (mate_row + n_row - 2 * j) % n_row)
        remote(src, src, s_vc.at[p, j], r_vc.at[p, j], mate_row, col).wait_recv()

    def block_copy(n):
        src = gmid_ref if n == 1 else ginv_ref.at[n // 2]
        dst = pmid if n == 1 else pinv.at[n // 2]
        return remote(src, dst, s_g.at[n], r_g.at[n], row, mate_col)

    depth = chunk * tile
    chunks = rounds // chunk
    first = 1 - row // 2 if local else 0
    blocks = (chunks - 1 if local else chunks) * tiles

    def values(p, c):
        return solved_rows[p, pl.ds(c * chunk, chunk)].reshape(depth, wide)

    def add(p, a, c, block, fresh):
        count = block.shape[0] // tile
        got = jnp.dot(block, values(p, c), preferred_element_type=F32).reshape(count, tile, wide)
        where = (pl.ds(a, count), slice(None), pl.ds(p * wide, wide))
        if fresh:
            pre_ref[where] = got
        else:
            pre_ref[where] += got

    def fetch(a, c, slot):
        at = pl.multiple_of(c * chunk, chunk)
        return pltpu.make_async_copy(left_ref.at[a, :, pl.ds(at, chunk), :], left_buf.at[slot], l_left.at[slot])

    def local_product():
        c = (row // 2) * (chunks - 1)
        fetch(0, c, 0).start()

        def step(a, carry):
            slot = a % 2

            @pl.when(a + 1 < tiles)
            def _():
                fetch(a + 1, c, 1 - slot).start()

            fetch(a, c, slot).wait()
            block = left_buf[slot].reshape(tile, depth)
            for p in range(PIECES):
                add(p, a, c, block, True)
            return carry

        lax.fori_loop(0, tiles, step, 0)

    def save(s, slot):
        return pltpu.make_async_copy(flat_buf.at[slot, 0], flat_ref.at[s], l_flat.at[slot])

    def rearrange(low, high, p):
        count = high - low

        def get(n, slot):
            s = low + n
            return fetch(s % tiles, first + s // tiles, slot)

        get(0, 0).start()

        def step(n, carry):
            slot = n % 2
            s = low + n

            @pl.when(n + 1 < count)
            def _():
                get(n + 1, 1 - slot).start()

            get(n, slot).wait()

            @pl.when(n >= 2)
            def _():
                save(s - 2, slot).wait()

            block = left_buf[slot].reshape(tile, depth)
            flat_buf[slot, 0] = block
            save(s, slot).start()
            if p is not None:
                add(p, s % tiles, first + s // tiles, block, not local)
            return carry

        lax.fori_loop(0, count, step, 0)
        save(high - 2, (count - 2) % 2).wait()
        save(high - 1, (count - 1) % 2).wait()

    def replay(low, high, p):
        count = (high - low) // 2

        def get(n, slot):
            return pltpu.make_async_copy(flat_ref.at[pl.ds(low + 2 * n, 2)], flat_buf.at[slot], l_flat.at[slot])

        get(0, 0).start()

        def step(n, carry):
            slot = n % 2

            @pl.when(n + 1 < count)
            def _():
                get(n + 1, 1 - slot).start()

            get(n, slot).wait()
            s = low + 2 * n
            add(p, s % tiles, first + s // tiles, flat_buf[slot].reshape(2 * tile, depth), not local)
            return carry

        lax.fori_loop(0, count, step, 0)

    def bring(p):
        for j in range(1, band):
            cross_wait(p, j)
            hand_copy(p, j).start()
        if p + 1 < PIECES:
            for j in range(1, band):
                cross_copy(p, j).wait_send()
            for j in range(1, band):
                cross_copy(p + 1, j).start()
        for j in range(1, band):
            hand_wait(p, j)

    def first_sum(p):
        pair_copy(0, p).wait_recv()
        for a in range(half):
            part[p, a] = pair_sum(0, p, a)
        send_parts(0, p)

    def advance(f, p):
        take(f, p)
        if f < 3:
            apply(f + 1, p)
            send_parts(f + 1, p)

    for p in range(PIECES):
        own_copy(p).wait()
        hand_copy(p, 0).start()
        if p == 0:
            for j in range(1, band):
                cross_copy(p, j).start()
    for n in range(3):
        block_copy(n).start()
    for p in range(PIECES):
        hand_wait(p, 0)
    middle = blocks // 2
    if local:
        local_product()
    rearrange(0, middle, None)
    bring(0)
    rearrange(middle, blocks, 0)
    replay(0, middle, 0)
    pair_start(0)
    first_sum(0)
    bring(1)
    replay(0, middle, 1)
    advance(0, 0)
    replay(middle, blocks, 1)
    pair_start(1)
    advance(1, 0)
    first_sum(1)
    advance(2, 0)
    advance(0, 1)
    advance(3, 0)
    advance(1, 1)
    gather_on(0, 0)
    advance(2, 1)
    gather_on(0, 1)
    gather_on(1, 0)
    gather_end(0, 0)
    gather_end(1, 0)
    advance(3, 1)
    gather_end(0, 1)
    cov_all[...] = outer(0)
    gather_on(1, 1)
    gather_end(1, 1)
    cov_all[...] += outer(1)

    rows = pl.ds(pl.multiple_of(col * share % 128, share), share)
    own_cov = cov_all[rows, :]
    cov_out[...] = own_cov.astype(BF16)

    def cov_copy(j):
        return remote(cov_out, cov_in.at[j - 1], s_cov.at[j - 1], r_cov.at[j - 1], (row + j) % n_row, col)

    for j in range(1, n_row):
        cov_copy(j).start()
    total = own_cov
    for j in range(1, n_row):
        cov_copy(j).wait_recv()
        total = total + cov_in[j - 1].astype(F32)
    cov_ref[...] = prior_ref[...] - total / total_rows

    for j in range(1, n_row):
        cov_copy(j).wait_send()
    for n in range(3):
        block_copy(n).wait_send()
    for j in range(1, band):
        cross_copy(PIECES - 1, j).wait_send()
    for p in range(PIECES):
        for j in range(band):
            hand_copy(p, j).wait_send()
    for p in range(PIECES):
        for panel in range(2):
            pair_copy(panel, p).wait_send()
            for i in range(owners):
                forward_copy(panel, p, i).wait_send()
        for f in range(4):
            for i in range(owners):
                @pl.when(not_owner(i))
                def _():
                    reduce_copy(f, p, i).wait_send()
            if f < 3:
                core_copy(f, p).wait_send()

        @pl.when(active)
        def _():
            for f in range(3):
                for j in range(1, band):
                    x_copy(f, p, j).wait_send()
            for g in range(2):
                for dz in range(1, n_z):
                    gather_copy(g, p, dz).wait_send()


def chain(n_row, n_col, left, prev, cross, inverses, coupling, prior):
    tiles, tile, rounds, _ = left.shape
    sites = prev.shape[2]
    half, n_z, owners, band = tiles // 2, n_col // 2, n_col // n_row, n_row // 2
    per = half // owners
    width = sites // 2 // PIECES
    share = prior.shape[0]
    local = band == 2 and rounds % 16 == 0 and rounds >= 32
    chunk = 16 if local else rounds
    blocks = (rounds // chunk - (1 if local else 0)) * tiles
    dma = pltpu.SemaphoreType.DMA
    vm = pl.BlockSpec(memory_space=pltpu.VMEM)
    hbm = pl.BlockSpec(memory_space=pl.ANY)
    return pl.pallas_call(
        functools.partial(chain_kernel, n_row, n_col, chunk, local, tiles * tile * n_row),
        out_shape=(
            jax.ShapeDtypeStruct((tiles, tile, sites), BF16),
            jax.ShapeDtypeStruct((share, sites), F32),
            jax.ShapeDtypeStruct((blocks, tile, chunk * tile), BF16),
        ),
        in_specs=[hbm, hbm] + [vm] * 4,
        out_specs=(vm, vm, hbm),
        scratch_shapes=[
            pltpu.VMEM((tiles, tile, sites), F32),
            pltpu.VMEM((PIECES, rounds, tile, 2 * width), BF16),
            pltpu.VMEM((2, tile, chunk, tile), BF16),
            pltpu.VMEM((2, 2, tile, chunk * tile), BF16),
            pltpu.VMEM(inverses.shape, BF16),
            pltpu.VMEM(coupling.shape, BF16),
            pltpu.VMEM((PIECES, half, tile, width), F32),
            pltpu.VMEM((4, PIECES, owners, per, tile, width), BF16),
            pltpu.VMEM((4, PIECES, n_z - 1, per, tile, width), BF16),
            pltpu.VMEM((3, PIECES, 2, per, tile, width), BF16),
            pltpu.VMEM((2, 2, PIECES, owners, per, tile, width), BF16),
            pltpu.VMEM((2, PIECES, half, tile, width), BF16),
            pltpu.VMEM((2, PIECES, half, tile, width), BF16),
            pltpu.VMEM((share, sites), BF16),
            pltpu.VMEM((n_row - 1, share, sites), BF16),
            pltpu.VMEM((128, sites), F32),
            dma((2, PIECES)), dma((2, PIECES)),
            dma((4, PIECES, owners)), dma((4, PIECES, n_z - 1)),
            dma((3, PIECES, max(band - 1, 1))), dma((3, PIECES)),
            dma((3, PIECES)), dma((3, PIECES)),
            dma((2, PIECES, n_z - 1)), dma((2, PIECES, owners)),
            dma((2, PIECES, owners)), dma((2, PIECES, owners)),
            dma((n_row - 1,)), dma((n_row - 1,)),
            dma((PIECES,)), dma((2,)), dma((2,)),
            dma((PIECES, max(band - 1, 1))), dma((PIECES, max(band - 1, 1))),
            dma((PIECES, band)), dma((PIECES, band)),
            dma((3,)), dma((3,)),
        ],
        compiler_params=pltpu.CompilerParams(
            collective_id=0, has_side_effects=True, vmem_limit_bytes=60 * 1024 * 1024),
    )(left, prev, cross, inverses, coupling, prior)[:2]


def body(n_row, n_col, left_factor, prev_solution, cross, inverses, coupling, prior_cov):
    half, tile, cols, _ = coupling.shape
    return chain(
        n_row, n_col, left_factor, prev_solution, cross,
        inverses.reshape(2, half * tile, cols * tile), coupling.reshape(half * tile, cols * tile), prior_cov)


def solution(mesh):
    placed = (
        P(None, "row", None, "col"),
        P("row", "col", None),
        P(None, "row", None),
        P(None, None, "row", None, "col"),
        P(None, "row", None, "col"),
        P("col", None),
    )
    return jax.shard_map(
        functools.partial(body, mesh.shape["row"], mesh.shape["col"]),
        mesh=mesh,
        in_specs=placed,
        out_specs=(P(None, "row", None), P("col", None)),
        check_vma=False,
    )
```
